32 devices in a mesh: row: 4 (over y, core), col: 8 (over z, x).
Axes of the slice: x: 2, y: 2, z: 4, core: 2. Of those that a mesh axis runs over, the one named last changes fastest.
Arguments:
- cotangent: bfloat16 [8, 128, 16384], P(None, 'row', 'col'), may hold values from -6 to 6
- pre_act: bfloat16 [8, 128, 16384], P(None, 'row', 'col'), may hold values from -6 to 6
- kernel_one: bfloat16 [576, 64], replicated, may hold values from -0.25 to 0.25
- kernel_two: bfloat16 [576, 64], replicated, may hold values from -0.25 to 0.25
- offsets: int32 [2, 8, 128, 256], P(None, None, 'row', 'col'), may hold values from 0 to 62, as said below
- fractions: int32 [2, 8, 128, 256], P(None, None, 'row', 'col'), may hold values from 0 to 15
- anchors: int32 [2, 8, 4, 8], P(None, None, 'row', 'col'), may hold values from -1 to 0
Outputs:
- grad_ref: float32 [8, 128, 16384], P(None, 'row', 'col')
The draws below stay inside these ranges and needn't reach their ends.
Inputs may be any that keep to these rules, and one draw needn't show every extreme that they name: offsets index rows and columns of the (64) x (64) region of a tile.
All inputs are finite; a program needn't handle non-finite values.
Results may differ from the reference program's by a relative error of at most 0.0044.
Values may be sent and summed in bfloat16 or wider, within the bound.
A program may use at most 128 MiB of HBM per device.

```python
import jax
import jax.numpy as jnp
from jax import lax

C = 64
TILE = 32
FRAMES = 8
H = 128
W = 256
N_ROW = 4
N_COL = 8


def draw_offsets(key, part):
    motion_key, jitter_key = jax.random.split(jax.random.fold_in(key, 17))
    shape = (2, FRAMES, H, W)
    motion = jax.random.randint(motion_key, (2, FRAMES, H // TILE, W // TILE), 0, TILE, dtype=jnp.int32)
    motion = jnp.repeat(jnp.repeat(motion, TILE, axis=2), TILE, axis=3)
    which = lax.broadcasted_iota(jnp.int32, shape, 0)
    pos_y = lax.broadcasted_iota(jnp.int32, shape, 2) % TILE
    pos_x = lax.broadcasted_iota(jnp.int32, shape, 3) % TILE
    position = jnp.where(which == 0, pos_y, pos_x)
    jitter = jax.random.randint(jitter_key, shape, -3, 4, dtype=jnp.int32)
    return jnp.clip(position + motion + jitter, 0, 2 * TILE - 2).astype(jnp.int32)


def plant(entries, key, smallest, largest):
    extent = entries.shape
    place = [jax.random.randint(jax.random.fold_in(key, axis), (), 0, extent[axis]) for axis in range(len(extent))]
    entries = entries.at[tuple(place)].set(smallest)
    longest = extent.index(max(extent))
    place[longest] = (place[longest] + 1) % extent[longest]
    return entries.at[tuple(place)].set(largest)


def shard_levels(key, dims, pieces, smallest, top_value):
    def one(axis_at, shards_of):
        heights = jax.random.uniform(jax.random.fold_in(jax.random.fold_in(key, 6), axis_at), (shards_of,), jnp.float32, smallest / len(pieces), top_value / len(pieces))
        return jnp.repeat(jnp.exp(heights), dims[axis_at] // shards_of).reshape((-1,) + (1,) * (len(dims) - axis_at - 1))

    gain = one(*pieces[0])
    for cut in pieces[1:]:
        gain = gain * one(*cut)
    return gain


def normal_values(rng, extent, deviation, bound, cuts=(), kind=jnp.bfloat16):
    entries = jax.random.normal(rng, extent, jnp.float32) * deviation
    if len(cuts) > 0:
        entries = shard_levels(rng, extent, cuts, -0.22, 0.18) * entries
    return jnp.clip(entries, min=-bound, max=bound).astype(kind)


def setup_inputs(seed: int = 0) -> dict:
    seeds = jax.random.split(jax.random.key(seed), 8)
    return {
        "cotangent": normal_values(seeds[0], (FRAMES, H, W * C), 1.0, 6.0, ((1, 4), (2, 8))),
        "pre_act": normal_values(seeds[1], (FRAMES, H, W * C), 1.0, 6.0, ((1, 4), (2, 8))),
        "kernel_one": normal_values(seeds[2], (9 * C, C), (9 * C) ** -0.5, 0.25),
        "kernel_two": normal_values(seeds[3], (9 * C, C), (9 * C) ** -0.5, 0.25),
        "offsets": draw_offsets(jax.random.fold_in(seeds[7], 71), 0),
        "fractions": plant(jax.random.randint(seeds[5], (2, FRAMES, H, W), 0, 16), jax.random.fold_in(seeds[5], 1), 0, 15).astype(jnp.int32),
        "anchors": plant(jax.random.randint(seeds[6], (2, FRAMES, N_ROW, N_COL), -1, 1), jax.random.fold_in(seeds[6], 1), -1, 0).astype(jnp.int32),
    }


def kernel_blocks(kernel):
    return [[kernel[(3 * shift_y + shift_x) * C:(3 * shift_y + shift_x + 1) * C] for shift_x in range(3)] for shift_y in range(3)]

def back_conv(field, kernel):
    blocks = kernel_blocks(kernel)
    padded = jnp.pad(field, ((1, 1), (1, 1), (0, 0)))
    summed = jnp.zeros((H * W, C), jnp.float32)
    for shift_y in range(3):
        for shift_x in range(3):
            shifted = padded[2 - shift_y:2 - shift_y + H, 2 - shift_x:2 - shift_x + W].reshape(H * W, C)
            summed = summed + jnp.dot(shifted, blocks[shift_y][shift_x].T, preferred_element_type=jnp.float32)
    return summed.reshape(H, W, C)

def tile_region(warped_tile, offset_tile, fraction_tile):
    region_w = 2 * TILE
    frac_y = fraction_tile[0].astype(jnp.float32) / 16.0
    frac_x = fraction_tile[1].astype(jnp.float32) / 16.0
    values = warped_tile.astype(jnp.float32)
    index_list = []
    update_list = []
    for corner_y in range(2):
        for corner_x in range(2):
            weight_y = frac_y if corner_y == 1 else 1.0 - frac_y
            weight_x = frac_x if corner_x == 1 else 1.0 - frac_x
            flat_index = ((offset_tile[0] + corner_y) * region_w + offset_tile[1] + corner_x).reshape(-1)
            updates = ((weight_y * weight_x)[:, :, None] * values).reshape(-1, C)
            index_list.append(flat_index.astype(jnp.int32))
            update_list.append(updates)
    region = jax.ops.segment_sum(jnp.concatenate(update_list, axis=0), jnp.concatenate(index_list, axis=0), num_segments=region_w * region_w)
    return region.reshape(region_w, region_w, C)

def reference(cotangent, pre_act, kernel_one, kernel_two, offsets, fractions, anchors):

    def frame_grad(frame_pair):
        grad_frame = frame_pair[0].reshape(H, W, C)
        pre_frame = frame_pair[1].reshape(H, W, C)
        hidden = (back_conv(grad_frame, kernel_two) * (pre_frame > 0).astype(jnp.float32)).astype(jnp.bfloat16)
        return (grad_frame.astype(jnp.float32) + back_conv(hidden, kernel_one)).astype(jnp.bfloat16)
    warped_all = lax.map(frame_grad, (cotangent, pre_act))
    accumulator = jnp.zeros((FRAMES, H + 2 * TILE, W + 2 * TILE, C), jnp.float32)
    zero_at = jnp.zeros((), jnp.int32)

    def add_tile(tile_at, accumulator):
        tile_at = jnp.asarray(tile_at).astype(jnp.int32)
        frame_at = (tile_at // (N_ROW * N_COL)).astype(jnp.int32)
        row_at = (tile_at // N_COL % N_ROW).astype(jnp.int32)
        col_at = (tile_at % N_COL).astype(jnp.int32)
        warped_tile = lax.dynamic_slice(warped_all, (frame_at, row_at * TILE, col_at * TILE, zero_at), (1, TILE, TILE, C))[0]
        offset_tile = lax.dynamic_slice(offsets, (zero_at, frame_at, row_at * TILE, col_at * TILE), (2, 1, TILE, TILE))[:, 0]
        fraction_tile = lax.dynamic_slice(fractions, (zero_at, frame_at, row_at * TILE, col_at * TILE), (2, 1, TILE, TILE))[:, 0]
        region = tile_region(warped_tile, offset_tile, fraction_tile)
        rounded = lax.optimization_barrier(region.astype(jnp.bfloat16)).astype(jnp.float32)
        start_row = (TILE * (row_at + anchors[0, frame_at, row_at, col_at]) + TILE).astype(jnp.int32)
        start_col = (TILE * (col_at + anchors[1, frame_at, row_at, col_at]) + TILE).astype(jnp.int32)
        current = lax.dynamic_slice(accumulator, (frame_at, start_row, start_col, zero_at), (1, 2 * TILE, 2 * TILE, C))
        return lax.dynamic_update_slice(accumulator, current + rounded[None], (frame_at, start_row, start_col, zero_at))
    accumulator = lax.fori_loop(0, FRAMES * N_ROW * N_COL, add_tile, accumulator)
    return accumulator[:, TILE:TILE + H, TILE:TILE + W].reshape(FRAMES, H, W * C)
```

```python
import functools

import jax
import jax.numpy as jnp
from jax import lax
from jax.experimental import pallas as pl
from jax.experimental.pallas import tpu as pltpu
from jax.sharding import PartitionSpec as P

MESH = pl.DeviceIdType.MESH
ROWS = 48


def conv(lhs, b):
    y = jnp.dot(lhs, b, preferred_element_type=jnp.float32)
    return y


def kernel(
    n_row, n_col, frames,
    cot_ref, pre_ref, k2_ref, k1_ref, off_ref, frac_ref, tab_ref,
    out_ref,
    b2_ref, b1_ref, meta_scr, turn_scr,
    strips, strip_below, strip_above, halo, cot_right, cot_left, pre_right, pre_left, halo_right, halo_left,
    y_ref, hid_ref, w_ref, r_ref, pieces, below, above, to_left, to_right, from_right, from_left,
    tab_below, tab_above,
    row_send, row_recv, col_send, col_recv, tab_send, tab_recv,
    strip_send, strip_recv, side_send, side_recv,
):
    row = lax.axis_index("row")
    col = lax.axis_index("col")
    has_up, has_down = row > 0, row < n_row - 1
    has_left, has_right = col > 0, col < n_col - 1
    sides = ((has_up, {"row": row - 1}), (has_down, {"row": row + 1}),
             (has_left, {"col": col - 1}), (has_right, {"col": col + 1}))

    barrier = pltpu.get_barrier_semaphore()
    for there, who in sides:
        @pl.when(there)
        def _():
            pl.semaphore_signal(barrier, inc=1, device_id=who, device_id_type=MESH)

    wide = cot_ref.shape[2]
    f32 = lambda x: x.astype(jnp.float32)
    line16 = lax.broadcasted_iota(jnp.int32, (16, wide), 0)
    for g in range(frames // 4):
        first = jnp.zeros((16, wide), jnp.float32)
        last = jnp.zeros((16, wide), jnp.float32)
        for i in range(4):
            f = 4 * g + i
            mine = (line16 >= 4 * i) & (line16 < 4 * i + 4)
            x = jnp.where(line16 < 2, f32(cot_ref[f, 0:16]), pltpu.roll(f32(pre_ref[f, 0:16]), 2, 0))
            first = jnp.where(mine, pltpu.roll(x, 4 * i, 0) if i else x, first)
            x = jnp.where(line16 >= 14, f32(cot_ref[f, 16:32]), pltpu.roll(f32(pre_ref[f, 16:32]), 14, 0))
            last = jnp.where(mine, pltpu.roll(x, 4 * i + 4, 0) if i < 3 else x, last)
        strips[0, g] = first.astype(jnp.bfloat16)
        strips[1, g] = last.astype(jnp.bfloat16)

    pl.semaphore_wait(barrier, sum(there.astype(jnp.int32) for there, _ in sides))

    def tab_copy(d):
        return pltpu.make_async_remote_copy(
            src_ref=tab_ref, dst_ref=(tab_below, tab_above)[d],
            send_sem=tab_send.at[d], recv_sem=tab_recv.at[d],
            device_id=sides[d][1], device_id_type=MESH)

    def row_copy(d, f):
        return pltpu.make_async_remote_copy(
            src_ref=pieces.at[f, d], dst_ref=(below, above)[d].at[f],
            send_sem=row_send.at[d, f], recv_sem=row_recv.at[d, f],
            device_id=sides[d][1], device_id_type=MESH)

    def col_copy(d, f):
        return pltpu.make_async_remote_copy(
            src_ref=(to_left, to_right)[d].at[f], dst_ref=(from_right, from_left)[d].at[f],
            send_sem=col_send.at[d, f], recv_sem=col_recv.at[d, f],
            device_id=sides[2 + d][1], device_id_type=MESH)

    def strip_copy(d):
        return pltpu.make_async_remote_copy(
            src_ref=strips.at[d], dst_ref=(strip_below, strip_above)[d],
            send_sem=strip_send.at[d], recv_sem=strip_recv.at[d],
            device_id=sides[d][1], device_id_type=MESH)

    def side_copy(d, which):
        lanes = pl.ds(0, 128) if d == 0 else pl.ds(wide - 128, 128)
        dst = ((cot_right, cot_left), (pre_right, pre_left), (halo_right, halo_left))[which][d]
        return pltpu.make_async_remote_copy(
            src_ref=(cot_ref, pre_ref, halo)[which].at[:, :, lanes], dst_ref=dst,
            send_sem=side_send.at[d, which], recv_sem=side_recv.at[d, which],
            device_id=sides[2 + d][1], device_id_type=MESH)

    for d in range(2):
        @pl.when(sides[d][0])
        def _():
            strip_copy(d).start()
            tab_copy(d).start()
    for d in range(2):
        @pl.when(sides[2 + d][0])
        def _():
            side_copy(d, 0).start()
            side_copy(d, 1).start()

    for there, refs in ((has_down, (strip_below, tab_below, below)), (has_up, (strip_above, tab_above, above)),
                        (has_right, (cot_right, pre_right, halo_right, from_right)),
                        (has_left, (cot_left, pre_left, halo_left, from_left))):
        @pl.when(jnp.logical_not(there))
        def _():
            for ref in refs:
                @pl.loop(0, ref.shape[0])
                def _(f):
                    ref[f] = jnp.zeros(ref.shape[1:], ref.dtype)

    c = k1_ref.shape[1]
    for k_ref, b_ref in ((k2_ref, b2_ref), (k1_ref, b1_ref)):
        b_ref[...] = jnp.zeros(b_ref.shape, jnp.bfloat16)
        for t_y in range(3):
            for t in range(3):
                at = (3 * (2 - t_y) + 2 - t) * c
                block = jnp.transpose(f32(k_ref[at : at + c])).astype(jnp.bfloat16)
                for o in range(4):
                    b_ref[(o + t) * c : (o + t + 1) * c, (4 * t_y + o) * c : (4 * t_y + o + 1) * c] = block

    for d in range(2):
        @pl.when(sides[1 - d][0])
        def _():
            strip_copy(d).wait_recv()
    for f in range(frames):
        g, i = f // 4, f % 4
        low, high = f32(strip_below[g]), f32(strip_above[g])
        low = pltpu.roll(low, 16 - 4 * i, 0) if i else low
        high = pltpu.roll(high, 12 - 4 * i, 0) if i < 3 else high
        halo[f] = jnp.where(line16 < 4, low, jnp.where(line16 >= 12, high, 0.0)).astype(jnp.bfloat16)
    for d in range(2):
        @pl.when(sides[2 + d][0])
        def _():
            side_copy(d, 2).start()
    for d in range(2):
        @pl.when(sides[3 - d][0])
        def _():
            for which in range(3):
                side_copy(d, which).wait_recv()

    def compute(f):
        lane = lax.broadcasted_iota(jnp.int32, (32, 128), 1)
        low_half = lane < 64
        half = jnp.where(low_half, 0.0, 1.0)
        line = lax.broadcasted_iota(jnp.int32, (16, 128), 0)

        def cot_block(j):
            if j < 0:
                return jnp.concatenate([cot_left[f], halo_left[f]], axis=0)
            if j == 16:
                return jnp.concatenate([cot_right[f], halo_right[f]], axis=0)
            if j > 16:
                return jnp.zeros((ROWS, 128), jnp.bfloat16)
            return jnp.concatenate([cot_ref[f, :, 128 * j : 128 * j + 128], halo[f, :, 128 * j : 128 * j + 128]], axis=0)

        def pre_block(j):
            if j < 0:
                tile, edge = pre_left[f], halo_left[f]
            elif j == 16:
                tile, edge = pre_right[f], halo_right[f]
            elif j > 16:
                return jnp.zeros((ROWS, 128), jnp.float32)
            else:
                tile, edge = pre_ref[f, :, 128 * j : 128 * j + 128], halo[f, :, 128 * j : 128 * j + 128]
            edge = f32(edge)
            edge = jnp.where(line == 0, pltpu.roll(edge, 14, 0), jnp.where(line == 15, pltpu.roll(edge, 2, 0), 0.0))
            return jnp.concatenate([f32(tile), edge], axis=0)

        lhs = jnp.concatenate([jnp.concatenate([cot_block(2 * k - 1), cot_block(2 * k), cot_block(2 * k + 1)], axis=1)
                               for k in range(9)], axis=0)
        y_ref[...] = conv(lhs, b2_ref[...])
        for k in range(9):
            rows = slice(ROWS * k, ROWS * k + ROWS)
            h = (pltpu.roll(y_ref[rows, 0:256], 1, 0) + y_ref[rows, 256:512]
                 + pltpu.roll(y_ref[rows, 512:768], ROWS - 1, 0))
            pre = jnp.concatenate([pre_block(2 * k - 1), pre_block(2 * k), pre_block(2 * k + 1)], axis=1)
            pre = pltpu.roll(pre, 320, 1)[:, 0:256]
            hid_ref[:, 256 * k : 256 * k + 256] = jnp.where(pre > 0, h, 0.0).astype(jnp.bfloat16)
        lhs = jnp.concatenate([hid_ref[:, 256 * k : 256 * k + 384] for k in range(8)], axis=0)
        y_ref[0 : 8 * ROWS] = conv(lhs, b1_ref[...])
        four = jnp.concatenate([f32(r[d, f]) for r in (off_ref, frac_ref) for d in range(2)], axis=0)
        turn_scr[...] = jnp.transpose(four)
        place = lax.broadcasted_iota(jnp.int32, (8, 128), 1)
        parts = [turn_scr[pl.ds(i, 8, stride=4), :] for i in range(4)]
        for d in range(4):
            tile = jnp.zeros((8, 128), jnp.float32)
            for i in range(4):
                x = pltpu.roll(parts[i], (32 * (i - d)) % 128, 1) if i != d else parts[i]
                tile = jnp.where((place >= 32 * i) & (place < 32 * i + 32), x, tile)
            for j in range(8):
                meta_scr[d : d + 1, 128 * j : 128 * j + 128] = tile[j : j + 1]
        m = meta_scr[...]
        oy, ox = m[0:1], m[1:2].astype(jnp.int32)
        fy = m[2:3] / 16.0
        fx = m[3:4] / 16.0
        pixels = ox.shape[1]
        r0 = jnp.transpose(jnp.broadcast_to((ox & 3).astype(jnp.float32), (128, pixels)))
        r1 = jnp.where(r0 == 3.0, 0.0, r0 + 1.0)
        for k in range(8):
            rows = slice(ROWS * k, ROWS * k + ROWS)
            w = (pltpu.roll(y_ref[rows, 0:256], 1, 0) + y_ref[rows, 256:512]
                 + pltpu.roll(y_ref[rows, 512:768], ROWS - 1, 0))[0:32]
            w = w + cot_ref[f, :, 256 * k : 256 * k + 256].astype(jnp.float32)
            w = w.astype(jnp.bfloat16).astype(jnp.float32)
            for i in range(2):
                part = w[:, 128 * i : 128 * i + 128]
                turned = pltpu.roll(part, 64, 1)
                for e in range(2):
                    both = jnp.where(low_half, turned, part) if e else jnp.where(low_half, part, turned)
                    at = 64 * (2 * k + i) + 32 * e
                    for b, r in enumerate((r0, r1)):
                        which = r[at : at + 32] - half
                        for s in range(2):
                            r_ref[1024 * b + at : 1024 * b + at + 32, 128 * s : 128 * s + 128] = (
                                jnp.where(which == 2.0 * s, both, 0.0).astype(jnp.bfloat16))
        span = lax.broadcasted_iota(jnp.int32, (64, pixels), 0).astype(jnp.float32)
        wy = jnp.maximum(1.0 - jnp.abs(span - (oy + fy)), 0.0).astype(jnp.bfloat16)
        group = lax.broadcasted_iota(jnp.int32, (16, pixels), 0)
        wx = (jnp.where((ox >> 2) == group, 1.0 - fx, 0.0), jnp.where(((ox + 1) >> 2) == group, fx, 0.0))
        for n in range(16):
            for b in range(2):
                line = jnp.broadcast_to(wx[b][n : n + 1], (16, pixels)).astype(jnp.bfloat16)
                w_ref[64 * n : 64 * n + 64, pixels * b : pixels * b + pixels] = (
                    wy * jnp.concatenate([line] * 4, axis=0))
        region = jnp.dot(w_ref[...], r_ref[...], preferred_element_type=jnp.float32).astype(jnp.bfloat16)
        for n in range(16):
            for q in range(2):
                pieces[f, q, n // 8, :, 256 * (n % 8) : 256 * (n % 8) + 256] = (
                    region[64 * n + 32 * q : 64 * n + 32 * q + 32])

    def merge(f):
        for d in range(2):
            @pl.when(sides[1 - d][0])
            def _():
                row_copy(d, f).wait_recv()
        own, low, high = tab_ref[f], tab_below[f], tab_above[f]

        def scalars(t):
            return t[0:1, 0:1], t[1:2, 0:1], t[2:3, 0:1], t[3:4, 0:1]

        lo_r, hi_r, lo_c, hi_c = scalars(own)
        b_r, _, b_lo, b_hi = scalars(low)
        _, a_r, a_lo, a_hi = scalars(high)
        b_lo, b_hi, a_lo, a_hi = b_r * b_lo, b_r * b_hi, a_r * a_lo, a_r * a_hi
        for k in range(8):
            s = slice(256 * k, 256 * k + 256)
            o = [hi_r * f32(pieces[f, 0, q, :, s]) + lo_r * f32(pieces[f, 1, q, :, s]) for q in range(2)]
            lo = [f32(below[f, q, :, s]) for q in range(2)]
            up = [f32(above[f, q, :, s]) for q in range(2)]
            to_left[f, :, s] = (lo_c * o[0] + b_lo * lo[0] + a_lo * up[0]).astype(jnp.bfloat16)
            to_right[f, :, s] = (hi_c * o[1] + b_hi * lo[1] + a_hi * up[1]).astype(jnp.bfloat16)
            out_ref[f, :, s] = (hi_c * o[0] + b_hi * lo[0] + a_hi * up[0]
                                + lo_c * o[1] + b_lo * lo[1] + a_lo * up[1])
        for d in range(2):
            @pl.when(sides[2 + d][0])
            def _():
                col_copy(d, f).start()

    @pl.loop(0, frames + 1)
    def _(step):
        @pl.when(step < frames)
        def _():
            compute(step)
            for d in range(2):
                @pl.when(sides[d][0])
                def _():
                    row_copy(d, step).start()

        @pl.when(step == 0)
        def _():
            for d in range(2):
                @pl.when(sides[1 - d][0])
                def _():
                    tab_copy(d).wait_recv()

        @pl.when(step > 0)
        def _():
            merge(step - 1)

    @pl.loop(0, frames)
    def _(f):
        for d in range(2):
            @pl.when(sides[3 - d][0])
            def _():
                col_copy(d, f).wait_recv()
        out_ref[f] += from_right[f].astype(jnp.float32) + from_left[f].astype(jnp.float32)

    for d in range(2):
        @pl.when(sides[d][0])
        def _():
            tab_copy(d).wait_send()
            strip_copy(d).wait_send()

        @pl.when(sides[2 + d][0])
        def _():
            for which in range(3):
                side_copy(d, which).wait_send()

    @pl.loop(0, frames)
    def _(f):
        for d in range(2):
            @pl.when(sides[d][0])
            def _():
                row_copy(d, f).wait_send()

            @pl.when(sides[2 + d][0])
            def _():
                col_copy(d, f).wait_send()


def shards(cotangent, pre_act, kernel_one, kernel_two, offsets, fractions, anchors):
    frames, h, wc = cotangent.shape
    c = kernel_one.shape[1]
    w = wc // c
    n_row, n_col = lax.axis_size("row"), lax.axis_size("col")
    a = jnp.transpose(anchors[:, :, 0, 0]).astype(jnp.float32)
    zero = jnp.zeros((frames, 4), jnp.float32)
    tab = jnp.concatenate([-a[:, :1], 1.0 + a[:, :1], -a[:, 1:], 1.0 + a[:, 1:], zero], axis=1)
    tab = jnp.broadcast_to(tab[:, :, None], (frames, 8, 128))
    bf = jnp.bfloat16
    vmem = pl.BlockSpec(memory_space=pltpu.VMEM)
    dma = pltpu.SemaphoreType.DMA
    return pl.pallas_call(
        functools.partial(kernel, n_row, n_col, frames),
        out_shape=jax.ShapeDtypeStruct((frames, h, wc), jnp.float32),
        in_specs=[vmem] * 7,
        out_specs=vmem,
        scratch_shapes=[
            pltpu.VMEM((6 * c, 12 * c), bf),
            pltpu.VMEM((6 * c, 12 * c), bf),
            pltpu.VMEM((8, h * w), jnp.float32),
            pltpu.VMEM((w, 128), jnp.float32),
            pltpu.VMEM((2, frames // 4, 16, wc), bf),
            pltpu.VMEM((frames // 4, 16, wc), bf),
            pltpu.VMEM((frames // 4, 16, wc), bf),
            pltpu.VMEM((frames, 16, wc), bf),
            pltpu.VMEM((frames, h, 128), bf),
            pltpu.VMEM((frames, h, 128), bf),
            pltpu.VMEM((frames, h, 128), bf),
            pltpu.VMEM((frames, h, 128), bf),
            pltpu.VMEM((frames, 16, 128), bf),
            pltpu.VMEM((frames, 16, 128), bf),
            pltpu.VMEM((9 * ROWS, 12 * c), jnp.float32),
            pltpu.VMEM((ROWS, wc + 256), bf),
            pltpu.VMEM((h * w, 2 * h * w), bf),
            pltpu.VMEM((2 * h * w, 4 * c), bf),
            pltpu.VMEM((frames, 2, 2, h, wc), bf),
            pltpu.VMEM((frames, 2, h, wc), bf),
            pltpu.VMEM((frames, 2, h, wc), bf),
            pltpu.VMEM((frames, h, wc), bf),
            pltpu.VMEM((frames, h, wc), bf),
            pltpu.VMEM((frames, h, wc), bf),
            pltpu.VMEM((frames, h, wc), bf),
            pltpu.VMEM((frames, 8, 128), jnp.float32),
            pltpu.VMEM((frames, 8, 128), jnp.float32),
            dma((2, frames)), dma((2, frames)), dma((2, frames)), dma((2, frames)),
            dma((2,)), dma((2,)), dma((2,)), dma((2,)), dma((2, 3)), dma((2, 3)),
        ],
        compiler_params=pltpu.CompilerParams(
            collective_id=0, has_side_effects=True, vmem_limit_bytes=48 * 1024 * 1024
        ),
    )(cotangent, pre_act, kernel_two, kernel_one, offsets, fractions, tab)


def solution(mesh):
    in_specs = (
        P(None, "row", "col"),
        P(None, "row", "col"),
        P(),
        P(),
        P(None, None, "row", "col"),
        P(None, None, "row", "col"),
        P(None, None, "row", "col"),
    )
    out_specs = P(None, "row", "col")
    return jax.shard_map(shards, mesh=mesh, in_specs=in_specs, out_specs=out_specs, check_vma=False)
```

```python
import functools

import jax
import jax.numpy as jnp
from jax import lax
from jax.experimental import pallas as pl
from jax.experimental.pallas import tpu as pltpu
from jax.sharding import PartitionSpec as P

MESH = pl.DeviceIdType.MESH
ROWS = 48


def conv(lhs, b):
    y = jnp.dot(lhs, b, preferred_element_type=jnp.float32)
    return y


def kernel(
    n_row, n_col, frames,
    cot_in, pre_in, off_in, frac_in, k2_ref, k1_ref, tab_ref,
    out_ref,
    cot_ref, pre_ref, off_ref, frac_ref,
    b2_ref, b1_ref, meta_scr, turn_scr,
    strips, strip_below, strip_above, halo, cot_right, cot_left, pre_right, pre_left, halo_right, halo_left,
    y_ref, hid_ref, w_ref, r_ref, pieces, below, above, to_left, to_right, from_right, from_left,
    tab_below, tab_above,
    row_send, row_recv, col_send, col_recv, tab_send, tab_recv,
    strip_send, strip_recv, side_send, side_recv, load_sem,
):
    loads = [pltpu.make_async_copy(src, dst, load_sem.at[i]) for i, (src, dst) in enumerate(
        ((cot_in, cot_ref), (pre_in, pre_ref), (off_in, off_ref), (frac_in, frac_ref)))]
    for load in loads:
        load.start()
    row = lax.axis_index("row")
    col = lax.axis_index("col")
    has_up, has_down = row > 0, row < n_row - 1
    has_left, has_right = col > 0, col < n_col - 1
    sides = ((has_up, {"row": row - 1}), (has_down, {"row": row + 1}),
             (has_left, {"col": col - 1}), (has_right, {"col": col + 1}))

    barrier = pltpu.get_barrier_semaphore()
    for there, who in sides:
        @pl.when(there)
        def _():
            pl.semaphore_signal(barrier, inc=1, device_id=who, device_id_type=MESH)

    loads[0].wait()
    loads[1].wait()
    wide = cot_ref.shape[2]
    f32 = lambda x: x.astype(jnp.float32)
    line16 = lax.broadcasted_iota(jnp.int32, (16, wide), 0)
    for g in range(frames // 4):
        first = jnp.zeros((16, wide), jnp.float32)
        last = jnp.zeros((16, wide), jnp.float32)
        for i in range(4):
            f = 4 * g + i
            mine = (line16 >= 4 * i) & (line16 < 4 * i + 4)
            x = jnp.where(line16 < 2, f32(cot_ref[f, 0:16]), pltpu.roll(f32(pre_ref[f, 0:16]), 2, 0))
            first = jnp.where(mine, pltpu.roll(x, 4 * i, 0) if i else x, first)
            x = jnp.where(line16 >= 14, f32(cot_ref[f, 16:32]), pltpu.roll(f32(pre_ref[f, 16:32]), 14, 0))
            last = jnp.where(mine, pltpu.roll(x, 4 * i + 4, 0) if i < 3 else x, last)
        strips[0, g] = first.astype(jnp.bfloat16)
        strips[1, g] = last.astype(jnp.bfloat16)

    pl.semaphore_wait(barrier, sum(there.astype(jnp.int32) for there, _ in sides))

    def tab_copy(d):
        return pltpu.make_async_remote_copy(
            src_ref=tab_ref, dst_ref=(tab_below, tab_above)[d],
            send_sem=tab_send.at[d], recv_sem=tab_recv.at[d],
            device_id=sides[d][1], device_id_type=MESH)

    def row_copy(d, f):
        return pltpu.make_async_remote_copy(
            src_ref=pieces.at[f, d], dst_ref=(below, above)[d].at[f],
            send_sem=row_send.at[d, f], recv_sem=row_recv.at[d, f],
            device_id=sides[d][1], device_id_type=MESH)

    def col_copy(d, f):
        return pltpu.make_async_remote_copy(
            src_ref=(to_left, to_right)[d].at[f], dst_ref=(from_right, from_left)[d].at[f],
            send_sem=col_send.at[d, f], recv_sem=col_recv.at[d, f],
            device_id=sides[2 + d][1], device_id_type=MESH)

    def strip_copy(d):
        return pltpu.make_async_remote_copy(
            src_ref=strips.at[d], dst_ref=(strip_below, strip_above)[d],
            send_sem=strip_send.at[d], recv_sem=strip_recv.at[d],
            device_id=sides[d][1], device_id_type=MESH)

    def side_copy(d, which):
        lanes = pl.ds(0, 128) if d == 0 else pl.ds(wide - 128, 128)
        dst = ((cot_right, cot_left), (pre_right, pre_left), (halo_right, halo_left))[which][d]
        return pltpu.make_async_remote_copy(
            src_ref=(cot_ref, pre_ref, halo)[which].at[:, :, lanes], dst_ref=dst,
            send_sem=side_send.at[d, which], recv_sem=side_recv.at[d, which],
            device_id=sides[2 + d][1], device_id_type=MESH)

    for d in range(2):
        @pl.when(sides[d][0])
        def _():
            strip_copy(d).start()
            tab_copy(d).start()
    for d in range(2):
        @pl.when(sides[2 + d][0])
        def _():
            side_copy(d, 0).start()
            side_copy(d, 1).start()

    for there, refs in ((has_down, (strip_below, tab_below, below)), (has_up, (strip_above, tab_above, above)),
                        (has_right, (cot_right, pre_right, halo_right, from_right)),
                        (has_left, (cot_left, pre_left, halo_left, from_left))):
        @pl.when(jnp.logical_not(there))
        def _():
            for ref in refs:
                @pl.loop(0, ref.shape[0])
                def _(f):
                    ref[f] = jnp.zeros(ref.shape[1:], ref.dtype)

    c = k1_ref.shape[0]
    for k_ref, b_ref in ((k2_ref, b2_ref), (k1_ref, b1_ref)):
        b_ref[...] = jnp.zeros(b_ref.shape, jnp.bfloat16)
        for t_y in range(3):
            for t in range(3):
                at = (3 * (2 - t_y) + 2 - t) * c
                block = k_ref[:, at : at + c]
                for o in range(4):
                    b_ref[(o + t) * c : (o + t + 1) * c, (4 * t_y + o) * c : (4 * t_y + o + 1) * c] = block

    for d in range(2):
        @pl.when(sides[1 - d][0])
        def _():
            strip_copy(d).wait_recv()
    for f in range(frames):
        g, i = f // 4, f % 4
        low, high = f32(strip_below[g]), f32(strip_above[g])
        low = pltpu.roll(low, 16 - 4 * i, 0) if i else low
        high = pltpu.roll(high, 12 - 4 * i, 0) if i < 3 else high
        halo[f] = jnp.where(line16 < 4, low, jnp.where(line16 >= 12, high, 0.0)).astype(jnp.bfloat16)
    for d in range(2):
        @pl.when(sides[2 + d][0])
        def _():
            side_copy(d, 2).start()
    for d in range(2):
        @pl.when(sides[3 - d][0])
        def _():
            for which in range(3):
                side_copy(d, which).wait_recv()

    def compute(f):
        lane = lax.broadcasted_iota(jnp.int32, (32, 128), 1)
        low_half = lane < 64
        half = jnp.where(low_half, 0.0, 1.0)
        line = lax.broadcasted_iota(jnp.int32, (16, 128), 0)

        def cot_block(j):
            if j < 0:
                return jnp.concatenate([cot_left[f], halo_left[f]], axis=0)
            if j == 16:
                return jnp.concatenate([cot_right[f], halo_right[f]], axis=0)
            if j > 16:
                return jnp.zeros((ROWS, 128), jnp.bfloat16)
            return jnp.concatenate([cot_ref[f, :, 128 * j : 128 * j + 128], halo[f, :, 128 * j : 128 * j + 128]], axis=0)

        def pre_block(j):
            if j < 0:
                tile, edge = pre_left[f], halo_left[f]
            elif j == 16:
                tile, edge = pre_right[f], halo_right[f]
            elif j > 16:
                return jnp.zeros((ROWS, 128), jnp.float32)
            else:
                tile, edge = pre_ref[f, :, 128 * j : 128 * j + 128], halo[f, :, 128 * j : 128 * j + 128]
            edge = f32(edge)
            edge = jnp.where(line == 0, pltpu.roll(edge, 14, 0), jnp.where(line == 15, pltpu.roll(edge, 2, 0), 0.0))
            return jnp.concatenate([f32(tile), edge], axis=0)

        lhs = jnp.concatenate([jnp.concatenate([cot_block(2 * k - 1), cot_block(2 * k), cot_block(2 * k + 1)], axis=1)
                               for k in range(9)], axis=0)
        y_ref[...] = conv(lhs, b2_ref[...])
        for k in range(9):
            rows = slice(ROWS * k, ROWS * k + ROWS)
            h = (pltpu.roll(y_ref[rows, 0:256], 1, 0) + y_ref[rows, 256:512]
                 + pltpu.roll(y_ref[rows, 512:768], ROWS - 1, 0))
            pre = jnp.concatenate([pre_block(2 * k - 1), pre_block(2 * k), pre_block(2 * k + 1)], axis=1)
            pre = pltpu.roll(pre, 320, 1)[:, 0:256]
            hid_ref[:, 256 * k : 256 * k + 256] = jnp.where(pre > 0, h, 0.0).astype(jnp.bfloat16)
        lhs = jnp.concatenate([hid_ref[:, 256 * k : 256 * k + 384] for k in range(8)], axis=0)
        y_ref[0 : 8 * ROWS] = conv(lhs, b1_ref[...])
        four = jnp.concatenate([f32(r[d, f]) for r in (off_ref, frac_ref) for d in range(2)], axis=0)
        turn_scr[...] = jnp.transpose(four)
        place = lax.broadcasted_iota(jnp.int32, (8, 128), 1)
        parts = [turn_scr[pl.ds(i, 8, stride=4), :] for i in range(4)]
        for d in range(4):
            tile = jnp.zeros((8, 128), jnp.float32)
            for i in range(4):
                x = pltpu.roll(parts[i], (32 * (i - d)) % 128, 1) if i != d else parts[i]
                tile = jnp.where((place >= 32 * i) & (place < 32 * i + 32), x, tile)
            for j in range(8):
                meta_scr[d : d + 1, 128 * j : 128 * j + 128] = tile[j : j + 1]
        m = meta_scr[...]
        oy, ox = m[0:1], m[1:2].astype(jnp.int32)
        fy = m[2:3] / 16.0
        fx = m[3:4] / 16.0
        pixels = ox.shape[1]
        r0 = jnp.transpose(jnp.broadcast_to((ox & 3).astype(jnp.float32), (128, pixels)))
        r1 = jnp.where(r0 == 3.0, 0.0, r0 + 1.0)
        for k in range(8):
            rows = slice(ROWS * k, ROWS * k + ROWS)
            w = (pltpu.roll(y_ref[rows, 0:256], 1, 0) + y_ref[rows, 256:512]
                 + pltpu.roll(y_ref[rows, 512:768], ROWS - 1, 0))[0:32]
            w = w + cot_ref[f, :, 256 * k : 256 * k + 256].astype(jnp.float32)
            w = w.astype(jnp.bfloat16).astype(jnp.float32)
            for i in range(2):
                part = w[:, 128 * i : 128 * i + 128]
                turned = pltpu.roll(part, 64, 1)
                for e in range(2):
                    both = jnp.where(low_half, turned, part) if e else jnp.where(low_half, part, turned)
                    at = 64 * (2 * k + i) + 32 * e
                    for b, r in enumerate((r0, r1)):
                        which = r[at : at + 32] - half
                        for s in range(2):
                            r_ref[1024 * b + at : 1024 * b + at + 32, 128 * s : 128 * s + 128] = (
                                jnp.where(which == 2.0 * s, both, 0.0).astype(jnp.bfloat16))
        span = lax.broadcasted_iota(jnp.int32, (64, pixels), 0).astype(jnp.float32)
        wy = jnp.maximum(1.0 - jnp.abs(span - (oy + fy)), 0.0).astype(jnp.bfloat16)
        group = lax.broadcasted_iota(jnp.int32, (16, pixels), 0)
        wx = (jnp.where((ox >> 2) == group, 1.0 - fx, 0.0), jnp.where(((ox + 1) >> 2) == group, fx, 0.0))
        for n in range(16):
            for b in range(2):
                line = jnp.broadcast_to(wx[b][n : n + 1], (16, pixels)).astype(jnp.bfloat16)
                w_ref[64 * n : 64 * n + 64, pixels * b : pixels * b + pixels] = (
                    wy * jnp.concatenate([line] * 4, axis=0))
        region = jnp.dot(w_ref[...], r_ref[...], preferred_element_type=jnp.float32).astype(jnp.bfloat16)
        for n in range(16):
            for q in range(2):
                pieces[f, q, n // 8, :, 256 * (n % 8) : 256 * (n % 8) + 256] = (
                    region[64 * n + 32 * q : 64 * n + 32 * q + 32])

    def merge(f):
        for d in range(2):
            @pl.when(sides[1 - d][0])
            def _():
                row_copy(d, f).wait_recv()
        own, low, high = tab_ref[f], tab_below[f], tab_above[f]

        def scalars(t):
            return t[0:1, 0:1], t[1:2, 0:1], t[2:3, 0:1], t[3:4, 0:1]

        lo_r, hi_r, lo_c, hi_c = scalars(own)
        b_r, _, b_lo, b_hi = scalars(low)
        _, a_r, a_lo, a_hi = scalars(high)
        b_lo, b_hi, a_lo, a_hi = b_r * b_lo, b_r * b_hi, a_r * a_lo, a_r * a_hi
        for k in range(8):
            s = slice(256 * k, 256 * k + 256)
            o = [hi_r * f32(pieces[f, 0, q, :, s]) + lo_r * f32(pieces[f, 1, q, :, s]) for q in range(2)]
            lo = [f32(below[f, q, :, s]) for q in range(2)]
            up = [f32(above[f, q, :, s]) for q in range(2)]
            to_left[f, :, s] = (lo_c * o[0] + b_lo * lo[0] + a_lo * up[0]).astype(jnp.bfloat16)
            to_right[f, :, s] = (hi_c * o[1] + b_hi * lo[1] + a_hi * up[1]).astype(jnp.bfloat16)
            out_ref[f, :, s] = (hi_c * o[0] + b_hi * lo[0] + a_hi * up[0]
                                + lo_c * o[1] + b_lo * lo[1] + a_lo * up[1])
        for d in range(2):
            @pl.when(sides[2 + d][0])
            def _():
                col_copy(d, f).start()

    loads[2].wait()
    loads[3].wait()

    @pl.loop(0, frames + 1)
    def _(step):
        @pl.when(step < frames)
        def _():
            compute(step)
            for d in range(2):
                @pl.when(sides[d][0])
                def _():
                    row_copy(d, step).start()

        @pl.when(step == 0)
        def _():
            for d in range(2):
                @pl.when(sides[1 - d][0])
                def _():
                    tab_copy(d).wait_recv()

        @pl.when(step > 0)
        def _():
            merge(step - 1)

    @pl.loop(0, frames)
    def _(f):
        for d in range(2):
            @pl.when(sides[3 - d][0])
            def _():
                col_copy(d, f).wait_recv()
        out_ref[f] += from_right[f].astype(jnp.float32) + from_left[f].astype(jnp.float32)

    for d in range(2):
        @pl.when(sides[d][0])
        def _():
            tab_copy(d).wait_send()
            strip_copy(d).wait_send()

        @pl.when(sides[2 + d][0])
        def _():
            for which in range(3):
                side_copy(d, which).wait_send()

    @pl.loop(0, frames)
    def _(f):
        for d in range(2):
            @pl.when(sides[d][0])
            def _():
                row_copy(d, f).wait_send()

            @pl.when(sides[2 + d][0])
            def _():
                col_copy(d, f).wait_send()


def shards(cotangent, pre_act, kernel_one, kernel_two, offsets, fractions, anchors):
    frames, h, wc = cotangent.shape
    c = kernel_one.shape[1]
    w = wc // c
    n_row, n_col = lax.axis_size("row"), lax.axis_size("col")
    a = jnp.transpose(anchors[:, :, 0, 0]).astype(jnp.float32)
    zero = jnp.zeros((frames, 4), jnp.float32)
    tab = jnp.concatenate([-a[:, :1], 1.0 + a[:, :1], -a[:, 1:], 1.0 + a[:, 1:], zero], axis=1)
    tab = jnp.broadcast_to(tab[:, :, None], (frames, 8, 128))
    bf = jnp.bfloat16
    vmem = pl.BlockSpec(memory_space=pltpu.VMEM)
    dma = pltpu.SemaphoreType.DMA
    return pl.pallas_call(
        functools.partial(kernel, n_row, n_col, frames),
        out_shape=jax.ShapeDtypeStruct((frames, h, wc), jnp.float32),
        in_specs=[pl.BlockSpec(memory_space=pltpu.HBM)] * 4 + [vmem] * 3,
        out_specs=vmem,
        scratch_shapes=[
            pltpu.VMEM((frames, h, wc), bf),
            pltpu.VMEM((frames, h, wc), bf),
            pltpu.VMEM(offsets.shape, jnp.int32),
            pltpu.VMEM(fractions.shape, jnp.int32),
            pltpu.VMEM((6 * c, 12 * c), bf),
            pltpu.VMEM((6 * c, 12 * c), bf),
            pltpu.VMEM((8, h * w), jnp.float32),
            pltpu.VMEM((w, 128), jnp.float32),
            pltpu.VMEM((2, frames // 4, 16, wc), bf),
            pltpu.VMEM((frames // 4, 16, wc), bf),
            pltpu.VMEM((frames // 4, 16, wc), bf),
            pltpu.VMEM((frames, 16, wc), bf),
            pltpu.VMEM((frames, h, 128), bf),
            pltpu.VMEM((frames, h, 128), bf),
            pltpu.VMEM((frames, h, 128), bf),
            pltpu.VMEM((frames, h, 128), bf),
            pltpu.VMEM((frames, 16, 128), bf),
            pltpu.VMEM((frames, 16, 128), bf),
            pltpu.VMEM((9 * ROWS, 12 * c), jnp.float32),
            pltpu.VMEM((ROWS, wc + 256), bf),
            pltpu.VMEM((h * w, 2 * h * w), bf),
            pltpu.VMEM((2 * h * w, 4 * c), bf),
            pltpu.VMEM((frames, 2, 2, h, wc), bf),
            pltpu.VMEM((frames, 2, h, wc), bf),
            pltpu.VMEM((frames, 2, h, wc), bf),
            pltpu.VMEM((frames, h, wc), bf),
            pltpu.VMEM((frames, h, wc), bf),
            pltpu.VMEM((frames, h, wc), bf),
            pltpu.VMEM((frames, h, wc), bf),
            pltpu.VMEM((frames, 8, 128), jnp.float32),
            pltpu.VMEM((frames, 8, 128), jnp.float32),
            dma((2, frames)), dma((2, frames)), dma((2, frames)), dma((2, frames)),
            dma((2,)), dma((2,)), dma((2,)), dma((2,)), dma((2, 3)), dma((2, 3)), dma((4,)),
        ],
        compiler_params=pltpu.CompilerParams(
            collective_id=0, has_side_effects=True, vmem_limit_bytes=60 * 1024 * 1024
        ),
    )(cotangent, pre_act, offsets, fractions, kernel_two.T, kernel_one.T, tab)


def solution(mesh):
    in_specs = (
        P(None, "row", "col"),
        P(None, "row", "col"),
        P(),
        P(),
        P(None, None, "row", "col"),
        P(None, None, "row", "col"),
        P(None, None, "row", "col"),
    )
    out_specs = P(None, "row", "col")
    return jax.shard_map(shards, mesh=mesh, in_specs=in_specs, out_specs=out_specs, check_vma=False)
```

```python
import functools

import jax
import jax.numpy as jnp
from jax import lax
from jax.experimental import pallas as pl
from jax.experimental.pallas import tpu as pltpu
from jax.sharding import PartitionSpec as P

MESH = pl.DeviceIdType.MESH
ROWS = 48


def conv(lhs, b):
    y = jnp.dot(lhs, b, preferred_element_type=jnp.float32)
    return y


def kernel(
    n_row, n_col, frames,
    cot_in, pre_in, off_in, frac_in, k2_ref, k1_ref, tab_ref,
    out_ref,
    cot_ref, pre_ref, off_ref, frac_ref,
    b2_ref, b1_ref, meta_scr, turn_scr,
    strips, strip_below, strip_above, halo, cot_right, cot_left, pre_right, pre_left, halo_right, halo_left,
    y_ref, hid_ref, w_ref, r_ref, pieces, below, above, to_left, to_right, from_right, from_left,
    tab_below, tab_above,
    row_send, row_recv, col_send, col_recv, tab_send, tab_recv,
    strip_send, strip_recv, side_send, side_recv, load_sem,
):
    loads = [pltpu.make_async_copy(src, dst, load_sem.at[i]) for i, (src, dst) in enumerate(
        ((cot_in, cot_ref), (pre_in, pre_ref), (off_in, off_ref), (frac_in, frac_ref)))]
    for load in loads:
        load.start()
    row = lax.axis_index("row")
    col = lax.axis_index("col")
    has_up, has_down = row > 0, row < n_row - 1
    has_left, has_right = col > 0, col < n_col - 1
    sides = ((has_up, {"row": row - 1}), (has_down, {"row": row + 1}),
             (has_left, {"col": col - 1}), (has_right, {"col": col + 1}))

    barrier = pltpu.get_barrier_semaphore()
    for there, who in sides:
        @pl.when(there)
        def _():
            pl.semaphore_signal(barrier, inc=1, device_id=who, device_id_type=MESH)

    def spread_weights(k_ref, b_ref):
        c = k_ref.shape[0]
        b_ref[...] = jnp.zeros(b_ref.shape, jnp.bfloat16)
        for t_y in range(3):
            for t in range(3):
                at = (3 * (2 - t_y) + 2 - t) * c
                block = k_ref[:, at : at + c]
                for o in range(4):
                    b_ref[(o + t) * c : (o + t + 1) * c, (4 * t_y + o) * c : (4 * t_y + o + 1) * c] = block

    spread_weights(k2_ref, b2_ref)
    loads[0].wait()
    loads[1].wait()
    wide = cot_ref.shape[2]
    f32 = lambda x: x.astype(jnp.float32)
    line16 = lax.broadcasted_iota(jnp.int32, (16, wide), 0)
    for g in range(frames // 4):
        first = jnp.zeros((16, wide), jnp.float32)
        last = jnp.zeros((16, wide), jnp.float32)
        for i in range(4):
            f = 4 * g + i
            mine = (line16 >= 4 * i) & (line16 < 4 * i + 4)
            x = jnp.where(line16 < 2, f32(cot_ref[f, 0:16]), pltpu.roll(f32(pre_ref[f, 0:16]), 2, 0))
            first = jnp.where(mine, pltpu.roll(x, 4 * i, 0) if i else x, first)
            x = jnp.where(line16 >= 14, f32(cot_ref[f, 16:32]), pltpu.roll(f32(pre_ref[f, 16:32]), 14, 0))
            last = jnp.where(mine, pltpu.roll(x, 4 * i + 4, 0) if i < 3 else x, last)
        strips[0, g] = first.astype(jnp.bfloat16)
        strips[1, g] = last.astype(jnp.bfloat16)

    pl.semaphore_wait(barrier, sum(there.astype(jnp.int32) for there, _ in sides))

    def tab_copy(d):
        return pltpu.make_async_remote_copy(
            src_ref=tab_ref, dst_ref=(tab_below, tab_above)[d],
            send_sem=tab_send.at[d], recv_sem=tab_recv.at[d],
            device_id=sides[d][1], device_id_type=MESH)

    def row_copy(d, f):
        return pltpu.make_async_remote_copy(
            src_ref=pieces.at[f, d], dst_ref=(below, above)[d].at[f],
            send_sem=row_send.at[d, f], recv_sem=row_recv.at[d, f],
            device_id=sides[d][1], device_id_type=MESH)

    def col_copy(d, f):
        return pltpu.make_async_remote_copy(
            src_ref=(to_left, to_right)[d].at[f], dst_ref=(from_right, from_left)[d].at[f],
            send_sem=col_send.at[d, f], recv_sem=col_recv.at[d, f],
            device_id=sides[2 + d][1], device_id_type=MESH)

    def strip_copy(d):
        return pltpu.make_async_remote_copy(
            src_ref=strips.at[d], dst_ref=(strip_below, strip_above)[d],
            send_sem=strip_send.at[d], recv_sem=strip_recv.at[d],
            device_id=sides[d][1], device_id_type=MESH)

    def side_copy(d, which):
        lanes = pl.ds(0, 128) if d == 0 else pl.ds(wide - 128, 128)
        dst = ((cot_right, cot_left), (pre_right, pre_left), (halo_right, halo_left))[which][d]
        return pltpu.make_async_remote_copy(
            src_ref=(cot_ref, pre_ref, halo)[which].at[:, :, lanes], dst_ref=dst,
            send_sem=side_send.at[d, which], recv_sem=side_recv.at[d, which],
            device_id=sides[2 + d][1], device_id_type=MESH)

    for d in range(2):
        @pl.when(sides[d][0])
        def _():
            strip_copy(d).start()
            tab_copy(d).start()
    for d in range(2):
        @pl.when(sides[2 + d][0])
        def _():
            side_copy(d, 0).start()
            side_copy(d, 1).start()

    for there, refs in ((has_down, (strip_below, tab_below, below)), (has_up, (strip_above, tab_above, above)),
                        (has_right, (cot_right, pre_right, halo_right, from_right)),
                        (has_left, (cot_left, pre_left, halo_left, from_left))):
        @pl.when(jnp.logical_not(there))
        def _():
            for ref in refs:
                @pl.loop(0, ref.shape[0])
                def _(f):
                    ref[f] = jnp.zeros(ref.shape[1:], ref.dtype)

    spread_weights(k1_ref, b1_ref)

    for d in range(2):
        @pl.when(sides[1 - d][0])
        def _():
            strip_copy(d).wait_recv()
    for f in range(frames):
        g, i = f // 4, f % 4
        low, high = f32(strip_below[g]), f32(strip_above[g])
        low = pltpu.roll(low, 16 - 4 * i, 0) if i else low
        high = pltpu.roll(high, 12 - 4 * i, 0) if i < 3 else high
        halo[f] = jnp.where(line16 < 4, low, jnp.where(line16 >= 12, high, 0.0)).astype(jnp.bfloat16)
    for d in range(2):
        @pl.when(sides[2 + d][0])
        def _():
            side_copy(d, 2).start()
    for d in range(2):
        @pl.when(sides[3 - d][0])
        def _():
            for which in range(3):
                side_copy(d, which).wait_recv()

    def compute(f):
        lane = lax.broadcasted_iota(jnp.int32, (32, 128), 1)
        low_half = lane < 64
        half = jnp.where(low_half, 0.0, 1.0)
        line = lax.broadcasted_iota(jnp.int32, (16, 128), 0)

        def cot_block(j):
            if j < 0:
                return jnp.concatenate([cot_left[f], halo_left[f]], axis=0)
            if j == 16:
                return jnp.concatenate([cot_right[f], halo_right[f]], axis=0)
            if j > 16:
                return jnp.zeros((ROWS, 128), jnp.bfloat16)
            return jnp.concatenate([cot_ref[f, :, 128 * j : 128 * j + 128], halo[f, :, 128 * j : 128 * j + 128]], axis=0)

        def pre_block(j):
            if j < 0:
                tile, edge = pre_left[f], halo_left[f]
            elif j == 16:
                tile, edge = pre_right[f], halo_right[f]
            elif j > 16:
                return jnp.zeros((ROWS, 128), jnp.float32)
            else:
                tile, edge = pre_ref[f, :, 128 * j : 128 * j + 128], halo[f, :, 128 * j : 128 * j + 128]
            edge = f32(edge)
            edge = jnp.where(line == 0, pltpu.roll(edge, 14, 0), jnp.where(line == 15, pltpu.roll(edge, 2, 0), 0.0))
            return jnp.concatenate([f32(tile), edge], axis=0)

        lhs = jnp.concatenate([jnp.concatenate([cot_block(2 * k - 1), cot_block(2 * k), cot_block(2 * k + 1)], axis=1)
                               for k in range(9)], axis=0)
        y_ref[...] = conv(lhs, b2_ref[...])
        for k in range(9):
            rows = slice(ROWS * k, ROWS * k + ROWS)
            h = (pltpu.roll(y_ref[rows, 0:256], 1, 0) + y_ref[rows, 256:512]
                 + pltpu.roll(y_ref[rows, 512:768], ROWS - 1, 0))
            pre = jnp.concatenate([pre_block(2 * k - 1), pre_block(2 * k), pre_block(2 * k + 1)], axis=1)
            pre = pltpu.roll(pre, 320, 1)[:, 0:256]
            hid_ref[:, 256 * k : 256 * k + 256] = jnp.where(pre > 0, h, 0.0).astype(jnp.bfloat16)
        lhs = jnp.concatenate([hid_ref[:, 256 * k : 256 * k + 384] for k in range(8)], axis=0)
        y_ref[0 : 8 * ROWS] = conv(lhs, b1_ref[...])
        four = jnp.concatenate([f32(r[d, f]) for r in (off_ref, frac_ref) for d in range(2)], axis=0)
        turn_scr[...] = jnp.transpose(four)
        place = lax.broadcasted_iota(jnp.int32, (8, 128), 1)
        parts = [turn_scr[pl.ds(i, 8, stride=4), :] for i in range(4)]
        for d in range(4):
            tile = jnp.zeros((8, 128), jnp.float32)
            for i in range(4):
                x = pltpu.roll(parts[i], (32 * (i - d)) % 128, 1) if i != d else parts[i]
                tile = jnp.where((place >= 32 * i) & (place < 32 * i + 32), x, tile)
            for j in range(8):
                meta_scr[d : d + 1, 128 * j : 128 * j + 128] = tile[j : j + 1]
        m = meta_scr[...]
        oy, ox = m[0:1], m[1:2].astype(jnp.int32)
        fy = m[2:3] / 16.0
        fx = m[3:4] / 16.0
        pixels = ox.shape[1]
        r0 = jnp.transpose(jnp.broadcast_to((ox & 3).astype(jnp.float32), (128, pixels)))
        r1 = jnp.where(r0 == 3.0, 0.0, r0 + 1.0)
        for k in range(8):
            rows = slice(ROWS * k, ROWS * k + ROWS)
            w = (pltpu.roll(y_ref[rows, 0:256], 1, 0) + y_ref[rows, 256:512]
                 + pltpu.roll(y_ref[rows, 512:768], ROWS - 1, 0))[0:32]
            w = w + cot_ref[f, :, 256 * k : 256 * k + 256].astype(jnp.float32)
            w = w.astype(jnp.bfloat16).astype(jnp.float32)
            for i in range(2):
                part = w[:, 128 * i : 128 * i + 128]
                turned = pltpu.roll(part, 64, 1)
                for e in range(2):
                    both = jnp.where(low_half, turned, part) if e else jnp.where(low_half, part, turned)
                    at = 64 * (2 * k + i) + 32 * e
                    for b, r in enumerate((r0, r1)):
                        which = r[at : at + 32] - half
                        for s in range(2):
                            r_ref[1024 * b + at : 1024 * b + at + 32, 128 * s : 128 * s + 128] = (
                                jnp.where(which == 2.0 * s, both, 0.0).astype(jnp.bfloat16))
        span = lax.broadcasted_iota(jnp.int32, (64, pixels), 0).astype(jnp.float32)
        wy = jnp.maximum(1.0 - jnp.abs(span - (oy + fy)), 0.0).astype(jnp.bfloat16)
        group = lax.broadcasted_iota(jnp.int32, (16, pixels), 0)
        wx = (jnp.where((ox >> 2) == group, 1.0 - fx, 0.0), jnp.where(((ox + 1) >> 2) == group, fx, 0.0))
        for n in range(16):
            for b in range(2):
                line = jnp.broadcast_to(wx[b][n : n + 1], (16, pixels)).astype(jnp.bfloat16)
                w_ref[64 * n : 64 * n + 64, pixels * b : pixels * b + pixels] = (
                    wy * jnp.concatenate([line] * 4, axis=0))
        region = jnp.dot(w_ref[...], r_ref[...], preferred_element_type=jnp.float32).astype(jnp.bfloat16)
        for n in range(16):
            for q in range(2):
                pieces[f, q, n // 8, :, 256 * (n % 8) : 256 * (n % 8) + 256] = (
                    region[64 * n + 32 * q : 64 * n + 32 * q + 32])

    def merge(f):
        for d in range(2):
            @pl.when(sides[1 - d][0])
            def _():
                row_copy(d, f).wait_recv()
        own, low, high = tab_ref[f], tab_below[f], tab_above[f]

        def scalars(t):
            return t[0:1, 0:1], t[1:2, 0:1], t[2:3, 0:1], t[3:4, 0:1]

        lo_r, hi_r, lo_c, hi_c = scalars(own)
        b_r, _, b_lo, b_hi = scalars(low)
        _, a_r, a_lo, a_hi = scalars(high)
        b_lo, b_hi, a_lo, a_hi = b_r * b_lo, b_r * b_hi, a_r * a_lo, a_r * a_hi
        for k in range(8):
            s = slice(256 * k, 256 * k + 256)
            o = [hi_r * f32(pieces[f, 0, q, :, s]) + lo_r * f32(pieces[f, 1, q, :, s]) for q in range(2)]
            lo = [f32(below[f, q, :, s]) for q in range(2)]
            up = [f32(above[f, q, :, s]) for q in range(2)]
            to_left[f, :, s] = (lo_c * o[0] + b_lo * lo[0] + a_lo * up[0]).astype(jnp.bfloat16)
            to_right[f, :, s] = (hi_c * o[1] + b_hi * lo[1] + a_hi * up[1]).astype(jnp.bfloat16)
            out_ref[f, :, s] = (hi_c * o[0] + b_hi * lo[0] + a_hi * up[0]
                                + lo_c * o[1] + b_lo * lo[1] + a_lo * up[1])
        for d in range(2):
            @pl.when(sides[2 + d][0])
            def _():
                col_copy(d, f).start()

    loads[2].wait()
    loads[3].wait()

    @pl.loop(0, frames + 1)
    def _(step):
        @pl.when(step < frames)
        def _():
            compute(step)
            for d in range(2):
                @pl.when(sides[d][0])
                def _():
                    row_copy(d, step).start()

        @pl.when(step == 0)
        def _():
            for d in range(2):
                @pl.when(sides[1 - d][0])
                def _():
                    tab_copy(d).wait_recv()

        @pl.when(step > 0)
        def _():
            merge(step - 1)

    @pl.loop(0, frames)
    def _(f):
        for d in range(2):
            @pl.when(sides[3 - d][0])
            def _():
                col_copy(d, f).wait_recv()
        out_ref[f] += from_right[f].astype(jnp.float32) + from_left[f].astype(jnp.float32)

    for d in range(2):
        @pl.when(sides[d][0])
        def _():
            tab_copy(d).wait_send()
            strip_copy(d).wait_send()

        @pl.when(sides[2 + d][0])
        def _():
            for which in range(3):
                side_copy(d, which).wait_send()

    @pl.loop(0, frames)
    def _(f):
        for d in range(2):
            @pl.when(sides[d][0])
            def _():
                row_copy(d, f).wait_send()

            @pl.when(sides[2 + d][0])
            def _():
                col_copy(d, f).wait_send()


def shards(cotangent, pre_act, kernel_one, kernel_two, offsets, fractions, anchors):
    frames, h, wc = cotangent.shape
    c = kernel_one.shape[1]
    w = wc // c
    n_row, n_col = lax.axis_size("row"), lax.axis_size("col")
    a = jnp.transpose(anchors[:, :, 0, 0]).astype(jnp.float32)
    zero = jnp.zeros((frames, 4), jnp.float32)
    tab = jnp.concatenate([-a[:, :1], 1.0 + a[:, :1], -a[:, 1:], 1.0 + a[:, 1:], zero], axis=1)
    tab = jnp.broadcast_to(tab[:, :, None], (frames, 8, 128))
    bf = jnp.bfloat16
    vmem = pl.BlockSpec(memory_space=pltpu.VMEM)
    dma = pltpu.SemaphoreType.DMA
    return pl.pallas_call(
        functools.partial(kernel, n_row, n_col, frames),
        out_shape=jax.ShapeDtypeStruct((frames, h, wc), jnp.float32),
        in_specs=[pl.BlockSpec(memory_space=pltpu.HBM)] * 4 + [vmem] * 3,
        out_specs=vmem,
        scratch_shapes=[
            pltpu.VMEM((frames, h, wc), bf),
            pltpu.VMEM((frames, h, wc), bf),
            pltpu.VMEM(offsets.shape, jnp.int32),
            pltpu.VMEM(fractions.shape, jnp.int32),
            pltpu.VMEM((6 * c, 12 * c), bf),
            pltpu.VMEM((6 * c, 12 * c), bf),
            pltpu.VMEM((8, h * w), jnp.float32),
            pltpu.VMEM((w, 128), jnp.float32),
            pltpu.VMEM((2, frames // 4, 16, wc), bf),
            pltpu.VMEM((frames // 4, 16, wc), bf),
            pltpu.VMEM((frames // 4, 16, wc), bf),
            pltpu.VMEM((frames, 16, wc), bf),
            pltpu.VMEM((frames, h, 128), bf),
            pltpu.VMEM((frames, h, 128), bf),
            pltpu.VMEM((frames, h, 128), bf),
            pltpu.VMEM((frames, h, 128), bf),
            pltpu.VMEM((frames, 16, 128), bf),
            pltpu.VMEM((frames, 16, 128), bf),
            pltpu.VMEM((9 * ROWS, 12 * c), jnp.float32),
            pltpu.VMEM((ROWS, wc + 256), bf),
            pltpu.VMEM((h * w, 2 * h * w), bf),
            pltpu.VMEM((2 * h * w, 4 * c), bf),
            pltpu.VMEM((frames, 2, 2, h, wc), bf),
            pltpu.VMEM((frames, 2, h, wc), bf),
            pltpu.VMEM((frames, 2, h, wc), bf),
            pltpu.VMEM((frames, h, wc), bf),
            pltpu.VMEM((frames, h, wc), bf),
            pltpu.VMEM((frames, h, wc), bf),
            pltpu.VMEM((frames, h, wc), bf),
            pltpu.VMEM((frames, 8, 128), jnp.float32),
            pltpu.VMEM((frames, 8, 128), jnp.float32),
            dma((2, frames)), dma((2, frames)), dma((2, frames)), dma((2, frames)),
            dma((2,)), dma((2,)), dma((2,)), dma((2,)), dma((2, 3)), dma((2, 3)), dma((4,)),
        ],
        compiler_params=pltpu.CompilerParams(
            collective_id=0, has_side_effects=True, vmem_limit_bytes=60 * 1024 * 1024
        ),
    )(cotangent, pre_act, offsets, fractions, kernel_two.T, kernel_one.T, tab)


def solution(mesh):
    in_specs = (
        P(None, "row", "col"),
        P(None, "row", "col"),
        P(),
        P(),
        P(None, None, "row", "col"),
        P(None, None, "row", "col"),
        P(None, None, "row", "col"),
    )
    out_specs = P(None, "row", "col")
    return jax.shard_map(shards, mesh=mesh, in_specs=in_specs, out_specs=out_specs, check_vma=False)
```
